32 devices in a mesh: parts: 2 (over y), tile: 8 (over z, x), led: 2 (over core).
Axes of the slice: x: 2, y: 2, z: 4, core: 2. Of those that a mesh axis runs over, the one named last changes fastest.
Arguments:
- residual_spectra: bfloat16 [32, 2, 2048, 2048], P(('parts', 'led'), None, 'tile'), parts along dimension 0, may hold values from -6 to 6
- led_offsets: int32 [16, 2], P('led'), may hold values from -341 to 341
- pupil_radius: int32 [16], P('led'), may hold values from 409 to 512
- led_axial: float32 [16], P('led'), may hold values from 0.5 to 2
- depths: float32 [8], replicated, may hold values from -3 to 3
- slice_order: int32 [8], replicated, may hold values from 0 to 7, each once
- axial: float32 [2048, 2048], P('tile'), may hold values from 0 to 1.5
Outputs:
- gradient: float32 [16, 2, 2048, 2048], P('parts', None, ('tile', 'led')), parts along dimension 0
The draws below stay inside these ranges and needn't reach their ends.
There are 2 independent parts, one for each index of `parts`. The reference program is written for one: setup_inputs(seed, part) draws one part's arguments, and reference() takes and returns one part's arrays. A program takes and returns all parts, laid end to end along the dimension named above; an argument that names none is the same for every part. Nothing has to cross between parts.
Inputs may be any that keep to these rules, and one draw needn't show every extreme that they name: `slice_order`: each output slice names a different depth slice.
All inputs are finite; a program needn't handle non-finite values.
Results may differ from the reference program's by a relative error of at most 0.0057.
Values may be sent and summed in bfloat16 or wider, within the bound.
A program may use at most 256 MiB of HBM per device.

```python
import math
import jax
import jax.numpy as jnp
from jax import lax

N = 2048
SLICES = 8
LEDS = 16


def touch_ends(entries, stream_key, smallest, largest):
    spot = [jax.random.randint(jax.random.fold_in(stream_key, axis), (), 0, length) for axis, length in enumerate(entries.shape)]
    longest = entries.shape.index(max(entries.shape))
    beside = spot[:longest] + [(spot[longest] + 1) % entries.shape[longest]] + spot[longest + 1:]
    return entries.at[tuple(spot)].set(smallest).at[tuple(beside)].set(largest)


def steps_of(own_key, extent, split, least, high):
    loudness, own = 1.0, jax.random.fold_in(own_key, 6)
    for position, shards_of in split:
        draws = jnp.exp(jax.random.uniform(jax.random.fold_in(own, position), (shards_of,), jnp.float32, least / len(split), high / len(split)))
        loudness = loudness * jnp.repeat(draws, extent[position] // shards_of).reshape([-1 if axis == position else 1 for axis in range(len(extent))])
    return loudness


def noise(rng, extent, deviation, bound, shards=(), held_as=jnp.bfloat16):
    factor_of = steps_of(rng, extent, shards, -0.22, 0.18) if shards else 1.0
    array = jax.random.normal(rng, extent, jnp.float32) * deviation * factor_of
    return jnp.minimum(jnp.maximum(array, -bound), bound).astype(held_as)


def setup_inputs(seed: int = 0, part: int = 0) -> dict:
    arg_keys = jax.random.split(jax.random.key(seed), 8)
    own_keys = jax.random.split(jax.random.fold_in(arg_keys[7], part), 8)
    return {
        "residual_spectra": noise(own_keys[0], (LEDS, 2, N, N), 1.0, 6.0, ((0, 2), (2, 8))),
        "led_offsets": touch_ends(jax.random.randint(arg_keys[1], (LEDS, 2), 0 - N // 6, N // 6 + 1), jax.random.fold_in(arg_keys[1], 1), 0 - N // 6, (N // 6 + 1) - 1).astype(jnp.int32),
        "pupil_radius": touch_ends(jax.random.randint(arg_keys[2], (LEDS,), N // 5, N // 4 + 1), jax.random.fold_in(arg_keys[2], 1), N // 5, (N // 4 + 1) - 1).astype(jnp.int32),
        "led_axial": jnp.clip(0.5 + 1.5 * jax.random.uniform(arg_keys[3], (LEDS,), jnp.float32) ** steps_of(arg_keys[3], (LEDS,), ((0, 2),), -0.2, 0.2), 0.5, 2.0),
        "depths": jnp.clip(jax.random.uniform(arg_keys[4], (SLICES,), jnp.float32, -3.0, 3.0), -3.0, 3.0),
        "slice_order": jax.random.permutation(arg_keys[5], SLICES).astype(jnp.int32),
        "axial": jnp.clip(1.5 * jax.random.uniform(arg_keys[6], (N, N), jnp.float32) ** steps_of(arg_keys[6], (N, N), ((0, 8),), -0.2, 0.2), 0.0, 1.5),
    }


def signed_freq(index, length):
    return jnp.where(index < length // 2, index, index - length)


def dft_table(k_count, out_pos, length):
    k_index = jnp.arange(k_count, dtype=jnp.int32)
    phase_int = (k_index[:, None] * out_pos[None, :]) % length
    angles = phase_int.astype(jnp.float32) * (2.0 * math.pi / length)
    return jnp.stack([jnp.cos(angles), jnp.sin(angles)]).astype(jnp.bfloat16)


def masked_spectra(residual, offsets, radius, row_pos, length):
    freq_rows = signed_freq(row_pos, length)
    freq_cols = signed_freq(jnp.arange(length, dtype=jnp.int32), length)
    shift_rows = freq_rows[None, :] - offsets[:, 0:1]
    shift_cols = freq_cols[None, :] - offsets[:, 1:2]
    inside = shift_rows[:, :, None] ** 2 + shift_cols[:, None, :] ** 2 <= (radius ** 2)[:, None, None]
    return jnp.where(inside[:, None], residual, jnp.zeros_like(residual))


def select_depths(slice_order, depths):
    count = depths.shape[0]
    picker = (slice_order[:, None] == jnp.arange(count, dtype=jnp.int32)[None, :]).astype(jnp.float32)
    return jnp.dot(picker, depths, precision=lax.Precision.HIGHEST)


def mixing_weights(ordered, led_axial):
    phase_angle = ordered[:, None] * led_axial[None, :]
    cosine = jnp.cos(phase_angle)
    sine = jnp.sin(phase_angle)
    first = jnp.stack([cosine, sine], axis=-1)
    second = jnp.stack([-sine, cosine], axis=-1)
    return jnp.stack([first, second], axis=1).astype(jnp.bfloat16)


def apply_phase(summed, own_depths, axial):
    phase_angle = own_depths[:, None, None] * axial[None]
    cosine = jnp.cos(phase_angle)
    sine = jnp.sin(phase_angle)
    real_part = summed[:, 0] * cosine - summed[:, 1] * sine
    imag_part = summed[:, 0] * sine + summed[:, 1] * cosine
    return jnp.stack([real_part, imag_part], axis=1).astype(jnp.bfloat16)


def wide_transform(spectra, out_pos, length, form):
    dft = dft_table(spectra.shape[-1], out_pos, length)
    products = jnp.einsum(form, spectra.astype(jnp.float32), dft.astype(jnp.float32), precision=lax.Precision.HIGHEST)
    real_part = products[:, 0, 0] - products[:, 1, 1]
    imag_part = products[:, 0, 1] + products[:, 1, 0]
    return jnp.stack([real_part, imag_part], axis=1)


def reference(residual_spectra, led_offsets, pupil_radius, led_axial, depths, slice_order, axial):
    length = axial.shape[1]
    positions = jnp.arange(length, dtype=jnp.int32)
    masked = masked_spectra(residual_spectra, led_offsets, pupil_radius, positions, length)
    masked_wide = masked.astype(jnp.float32)
    ordered = select_depths(slice_order, depths)
    weights = mixing_weights(ordered, led_axial)

    def one_slice(inputs):
        weight, depth = inputs
        summed = jnp.einsum('olc,lcak->oak', weight.astype(jnp.float32), masked_wide, precision=lax.Precision.HIGHEST)
        phased = apply_phase(summed[None], depth[None], axial)
        half_done = wide_transform(phased, positions, length, 'jcak,tkm->jctma').astype(jnp.bfloat16)
        return wide_transform(half_done, positions, length, 'jcak,tkm->jctam')[0] * (1.0 / length)

    return lax.map(one_slice, (weights, ordered))
```

```python
import functools
import math

import jax
import jax.numpy as jnp
import ml_dtypes
import numpy as np
from jax import lax
from jax.experimental import pallas as pl
from jax.experimental.pallas import tpu as pltpu
from jax.sharding import PartitionSpec as P

LANES = 128
GROUP = 16
MESH = pl.DeviceIdType.MESH


def signed_freq(index, length):
    return jnp.where(index < length // 2, index, index - length)


def dft_table(k_count, out_pos, length):
    k_index = jnp.arange(k_count, dtype=jnp.int32)
    phase_int = k_index[:, None] * out_pos[None, :] % length
    angles = phase_int.astype(jnp.float32) * (2.0 * math.pi / length)
    return jnp.stack([jnp.cos(angles), jnp.sin(angles)]).astype(jnp.bfloat16)


def masked_spectra(residual, offsets, radius, row_pos, length):
    freq_rows = signed_freq(row_pos, length)
    freq_cols = signed_freq(jnp.arange(length, dtype=jnp.int32), length)
    shift_rows = freq_rows[None, :] - offsets[:, 0:1]
    shift_cols = freq_cols[None, :] - offsets[:, 1:2]
    inside = shift_rows[:, :, None] ** 2 + shift_cols[:, None, :] ** 2 <= (radius**2)[:, None, None]
    return jnp.where(inside[:, None], residual, jnp.zeros_like(residual))


def select_depths(slice_order, depths):
    count = depths.shape[0]
    picker = (slice_order[:, None] == jnp.arange(count, dtype=jnp.int32)[None, :]).astype(
        jnp.float32
    )
    return jnp.dot(picker, depths, precision=lax.Precision.HIGHEST)


def mixing_weights(ordered, led_axial):
    phase_angle = ordered[:, None] * led_axial[None, :]
    cosine = jnp.cos(phase_angle)
    sine = jnp.sin(phase_angle)
    first = jnp.stack([cosine, sine], axis=-1)
    second = jnp.stack([-sine, cosine], axis=-1)
    return jnp.stack([first, second], axis=1).astype(jnp.bfloat16)


def apply_phase(summed, own_depths, axial):
    phase_angle = own_depths[:, None, None] * axial[None]
    cosine = jnp.cos(phase_angle)
    sine = jnp.sin(phase_angle)
    real_part = summed[:, 0] * cosine - summed[:, 1] * sine
    imag_part = summed[:, 0] * sine + summed[:, 1] * cosine
    return jnp.stack([real_part, imag_part], axis=1).astype(jnp.bfloat16)


def transform(spectra, out_pos, length, form):
    dft = dft_table(spectra.shape[-1], out_pos, length)
    products = jnp.einsum(form, spectra, dft, preferred_element_type=jnp.float32)
    real_part = products[:, 0, 0] - products[:, 1, 1]
    imag_part = products[:, 0, 1] + products[:, 1, 0]
    return jnp.stack([real_part, imag_part], axis=1)


def column_section(spectra, out_pos, length):
    out_count = out_pos.shape[0]
    block_size = min(256, out_count)
    pieces = [
        transform(spectra, out_pos[start : start + block_size], length, "jcak,tkm->jctma")
        for start in range(0, out_count, block_size)
    ]
    return jnp.concatenate(pieces, axis=2).astype(jnp.bfloat16)


def row_section(spectra, length):
    positions = jnp.arange(length, dtype=jnp.int32)
    block_size = min(256, length)
    pieces = [
        transform(spectra, positions[start : start + block_size], length, "jcak,tkm->jctam")
        for start in range(0, length, block_size)
    ]
    return jnp.concatenate(pieces, axis=3) * (1.0 / length)


def local(residual_spectra, led_offsets, pupil_radius, led_axial, depths, slice_order, axial):
    tile_rows = axial.shape[0]
    length = axial.shape[1]
    row_pos = lax.axis_index("tile") * tile_rows + jnp.arange(tile_rows, dtype=jnp.int32)
    masked = masked_spectra(residual_spectra, led_offsets, pupil_radius, row_pos, length)
    ordered = select_depths(slice_order, depths)
    weights = mixing_weights(ordered, led_axial)
    partial_value = jnp.einsum(
        "jolc,lcak->joak", weights, masked, preferred_element_type=jnp.float32
    )
    led_count = lax.axis_size("led")
    led_index = lax.axis_index("led")
    slice_count = depths.shape[0]
    summed = lax.psum_scatter(partial_value, "led", scatter_dimension=0, tiled=True)
    own_count = slice_count // led_count
    own_depths = lax.dynamic_slice_in_dim(ordered, led_index * own_count, own_count)
    phased = apply_phase(summed, own_depths, axial)
    half_done = column_section(phased, jnp.arange(length, dtype=jnp.int32), length)
    regrouped = lax.all_to_all(
        lax.all_to_all(half_done, "tile", split_axis=2, concat_axis=3, tiled=True),
        "led",
        split_axis=2,
        concat_axis=0,
        tiled=True,
    )
    gradient = row_section(regrouped, length)
    return gradient


def full_table(length):
    phase_int = np.outer(np.arange(length), np.arange(length)) % length
    angles = np.arange(length).astype(np.float64) * (2.0 * math.pi / length)
    pair = np.stack([np.cos(angles), np.sin(angles)]).astype(np.float32).astype(ml_dtypes.bfloat16)
    return pair[:, phase_int]


def useful_edge(length):
    reach = length // 6 + length // 4
    return -(-(reach + 1) // LANES) * LANES


def sine_cosine(angle):
    quarter = angle * 0.25
    z = quarter * quarter
    sine = quarter * (1.0 + z * (-1 / 6 + z * (1 / 120 + z * (-1 / 5040 + z * (1 / 362880)))))
    cosine = 1.0 + z * (
        -1 / 2 + z * (1 / 24 + z * (-1 / 720 + z * (1 / 40320 - z * (1 / 3628800))))
    )
    for _ in range(2):
        sine, cosine = 2.0 * sine * cosine, 1.0 - 2.0 * sine * sine
    return sine, cosine


def mix_kernel(length, edge, ints, depths, weights, own, peer, axial, out):
    own_leds, peer_leds = own.shape[0], peer.shape[0]
    leds = own_leds + peer_leds
    slices = out.shape[0]
    row = ints[1] + pl.program_id(0) * GROUP + lax.broadcasted_iota(jnp.int32, (GROUP, 1), 0)
    freq_row = jnp.where(row < length // 2, row, row - length)
    lane = lax.broadcasted_iota(jnp.int32, (1, edge), 1)
    for half in range(2):
        start = 0 if half == 0 else length - edge
        freq_col = lane if half == 0 else lane - edge
        planes = []
        for led in range(leds):
            shift_row = freq_row - ints[2 + led]
            shift_col = freq_col - ints[2 + leds + led]
            room = ints[2 + 2 * leds + led] - shift_row * shift_row
            inside = jnp.where(shift_col * shift_col <= room, 1.0, 0.0).astype(jnp.bfloat16)
            for part in range(2):
                if led < own_leds:
                    values = own[led, part, :, start : start + edge]
                else:
                    values = peer[led - own_leds, part, :, half * edge : (half + 1) * edge]
                planes.append(values * inside)
        stacked = jnp.concatenate(planes, axis=0)
        summed = jnp.dot(weights[...], stacked, preferred_element_type=jnp.float32)
        wave = axial[:, start : start + edge]
        for j in range(slices):
            real = summed[(2 * j) * GROUP : (2 * j + 1) * GROUP]
            imag = summed[(2 * j + 1) * GROUP : (2 * j + 2) * GROUP]
            sine, cosine = sine_cosine(depths[j] * wave)
            where = slice(half * edge, (half + 1) * edge)
            out[j, 0, :, where] = (real * cosine - imag * sine).astype(jnp.bfloat16)
            out[j, 1, :, where] = (real * sine + imag * cosine).astype(jnp.bfloat16)


def transform_kernel(
    length,
    edge,
    table_hbm,
    phased_hbm,
    out_hbm,
    table,
    phased,
    send,
    recv,
    result,
    load_sem,
    phased_sem,
    send_sem,
    recv_sem,
    out_sem,
):
    slices = phased.shape[0]
    count = length // LANES
    dead_first, dead_last = edge // LANES, count - edge // LANES
    led_count = lax.axis_size("led")
    part = lax.axis_index("parts")
    me = lax.axis_index("tile") * led_count + lax.axis_index("led")

    def place(device):
        return (part, device // led_count, device % led_count)

    table_load = pltpu.make_async_copy(table_hbm, table, load_sem)
    table_load.start()
    phased_load = pltpu.make_async_copy(phased_hbm, phased, phased_sem)
    phased_load.start()

    barrier = pltpu.get_barrier_semaphore()

    @pl.loop(1, count)
    def _(step):
        pl.semaphore_signal(
            barrier, inc=1, device_id=place((me + step) % count), device_id_type=MESH
        )

    pl.semaphore_wait(barrier, count - 1)
    phased_load.wait()
    table_load.wait()

    def lanes_of(device):
        return pl.ds(pl.multiple_of(device * LANES, LANES), LANES)

    def remote(j, device):
        return pltpu.make_async_remote_copy(
            src_ref=send.at[j, device],
            dst_ref=recv.at[j, :, lanes_of(me)],
            send_sem=send_sem.at[j, device],
            recv_sem=recv_sem.at[j, me],
            device_id=place(device),
            device_id_type=MESH,
        )

    def landing(j, device):
        return pltpu.make_async_copy(
            send.at[j, device], recv.at[j, :, lanes_of(device)], recv_sem.at[j, device]
        )

    has_rows = jnp.logical_or(me < dead_first, me >= dead_last)
    quad = 4
    groups = count // quad

    @pl.when(has_rows)
    def _():
        @pl.loop(0, slices)
        def _(j):
            spectra = phased[j]

            @pl.loop(0, groups)
            def _(step):
                group = (me // quad + groups // 2 + step) % groups
                rows = pl.ds(pl.multiple_of(group * quad * LANES, quad * LANES), quad * LANES)

                def product(t):
                    values = jnp.concatenate(
                        [table[t, rows, :edge], table[t, rows, length - edge :]], axis=1
                    )
                    return lax.dot_general(
                        values,
                        spectra,
                        (((1,), (1,)), ((), ())),
                        preferred_element_type=jnp.float32,
                    )

                by_cosine = product(0)
                by_sine = product(1)
                real = (by_cosine[:, :LANES] - by_sine[:, LANES:]).astype(jnp.bfloat16)
                imag = (by_sine[:, :LANES] + by_cosine[:, LANES:]).astype(jnp.bfloat16)
                for q in range(quad):
                    device = group * quad + q
                    send[j, device, :LANES] = real[q * LANES : (q + 1) * LANES]
                    send[j, device, LANES:] = imag[q * LANES : (q + 1) * LANES]

                    @pl.when(device == me)
                    def _():
                        landing(j, me).start()

                    @pl.when(device != me)
                    def _():
                        remote(j, device).start()

    width = 512

    def write(j):
        return pltpu.make_async_copy(result.at[j % 2], out_hbm.at[j], out_sem.at[j % 2])

    @pl.loop(0, slices)
    def _(j):
        @pl.loop(0, dead_first)
        def _(source):
            landing(j, source).wait()

        @pl.loop(dead_last, count)
        def _(source):
            landing(j, source).wait()

        @pl.when(j >= 2)
        def _():
            write(j - 2).wait()

        @pl.loop(0, length // width)
        def _(block):
            cols = pl.ds(pl.multiple_of(block * width, width), width)
            spectra = jnp.concatenate(
                [recv[j, :, :edge], recv[j, :, length - edge :]], axis=1
            )

            def product(t):
                values = jnp.concatenate(
                    [table[t, :edge, cols], table[t, length - edge :, cols]], axis=0
                )
                return jnp.dot(spectra, values, preferred_element_type=jnp.float32)

            by_cosine = product(0)
            by_sine = product(1)
            scale = 1.0 / length
            result[j % 2, 0, :, cols] = (by_cosine[:LANES] - by_sine[LANES:]) * scale
            result[j % 2, 1, :, cols] = (by_sine[:LANES] + by_cosine[LANES:]) * scale

        write(j).start()

    write(slices - 2).wait()
    write(slices - 1).wait()

    @pl.when(has_rows)
    def _():
        @pl.loop(0, slices)
        def _(j):
            @pl.loop(1, count)
            def _(step):
                remote(j, (me + step) % count).wait_send()


def local_fast(residual_spectra, led_offsets, pupil_radius, led_axial, depths, slice_order, axial):
    tile_rows, length = axial.shape
    own_leds = residual_spectra.shape[0]
    slices = depths.shape[0]
    led_count = lax.axis_size("led")
    led_index = lax.axis_index("led")
    edge = useful_edge(length)
    rows = tile_rows // led_count
    swap = [(0, 1), (1, 0)]
    other = lax.dynamic_slice_in_dim(residual_spectra, (1 - led_index) * rows, rows, axis=2)
    other = jnp.concatenate([other[..., :edge], other[..., length - edge :]], axis=-1)
    peer = lax.ppermute(other, "led", swap)
    facts = jnp.concatenate(
        [led_offsets.astype(jnp.float32).T, pupil_radius.astype(jnp.float32)[None], led_axial[None]]
    )
    facts = jnp.concatenate([facts, lax.ppermute(facts, "led", swap)], axis=1)
    ordered = select_depths(slice_order, depths)
    weights = mixing_weights(ordered, facts[3])
    weights = weights.reshape(2 * slices, 2 * facts.shape[1])
    eye = jnp.eye(GROUP, dtype=jnp.bfloat16)
    weights = (weights[:, None, :, None] * eye[None, :, None, :]).reshape(
        2 * slices * GROUP, 2 * facts.shape[1] * GROUP
    )
    whole = facts[:3].astype(jnp.int32)
    first_row = lax.axis_index("tile") * tile_rows + led_index * rows
    ints = jnp.concatenate(
        [jnp.stack([led_index, first_row]), whole[0], whole[1], whole[2] * whole[2]]
    )
    steps = rows // GROUP
    phased = pl.pallas_call(
        functools.partial(mix_kernel, length, edge),
        grid_spec=pltpu.PrefetchScalarGridSpec(
            num_scalar_prefetch=2,
            grid=(steps,),
            in_specs=[
                pl.BlockSpec(weights.shape, lambda g, s, d: (0, 0)),
                pl.BlockSpec(
                    (own_leds, 2, GROUP, length), lambda g, s, d: (0, 0, s[0] * steps + g, 0)
                ),
                pl.BlockSpec((own_leds, 2, GROUP, 2 * edge), lambda g, s, d: (0, 0, g, 0)),
                pl.BlockSpec((GROUP, length), lambda g, s, d: (s[0] * steps + g, 0)),
            ],
            out_specs=pl.BlockSpec((slices, 2, GROUP, 2 * edge), lambda g, s, d: (0, 0, g, 0)),
        ),
        out_shape=jax.ShapeDtypeStruct((slices, 2, rows, 2 * edge), jnp.bfloat16),
        compiler_params=pltpu.CompilerParams(vmem_limit_bytes=48 * 2**20),
        name="mix",
    )(ints, ordered, weights, residual_spectra, peer, axial)
    phased = phased.reshape(slices, 2 * rows, 2 * edge)
    count = length // LANES
    bf16 = jnp.bfloat16
    return pl.pallas_call(
        functools.partial(transform_kernel, length, edge),
        in_specs=[pl.BlockSpec(memory_space=pl.ANY)] * 2,
        out_specs=pl.BlockSpec(memory_space=pl.ANY),
        out_shape=jax.ShapeDtypeStruct((slices, 2, LANES, length), jnp.float32),
        scratch_shapes=[
            pltpu.VMEM((2, length, length), bf16),
            pltpu.VMEM(phased.shape, bf16),
            pltpu.VMEM((slices, count, 2 * LANES, LANES), bf16),
            pltpu.VMEM((slices, 2 * LANES, length), bf16),
            pltpu.VMEM((2, 2, LANES, length), jnp.float32),
            pltpu.SemaphoreType.DMA,
            pltpu.SemaphoreType.DMA,
            pltpu.SemaphoreType.DMA((slices, count)),
            pltpu.SemaphoreType.DMA((slices, count)),
            pltpu.SemaphoreType.DMA((2,)),
        ],
        compiler_params=pltpu.CompilerParams(
            collective_id=0, has_side_effects=True, vmem_limit_bytes=60 * 2**20
        ),
        name="transform",
    )(jnp.asarray(full_table(length)), phased)


def local_any(*arrays):
    tile_rows, length = arrays[-1].shape
    led_count = lax.axis_size("led")
    if led_count == 2 and tile_rows == 2 * LANES and length % (8 * LANES) == 0:
        return local_fast(*arrays)
    return local(*arrays)


def solution(mesh):
    placed = (
        P(("parts", "led"), None, "tile", None),
        P("led", None),
        P("led"),
        P("led"),
        P(),
        P(),
        P("tile", None),
    )
    return jax.shard_map(
        local_any,
        mesh=mesh,
        in_specs=placed,
        out_specs=P("parts", None, ("tile", "led"), None),
        check_vma=False,
    )
```

```python
import functools
import math

import jax
import jax.numpy as jnp
import ml_dtypes
import numpy as np
from jax import lax
from jax.experimental import pallas as pl
from jax.experimental.pallas import tpu as pltpu
from jax.sharding import PartitionSpec as P

LANES = 128
GROUP = 16
MESH = pl.DeviceIdType.MESH


def signed_freq(index, length):
    return jnp.where(index < length // 2, index, index - length)


def dft_table(k_count, out_pos, length):
    k_index = jnp.arange(k_count, dtype=jnp.int32)
    phase_int = k_index[:, None] * out_pos[None, :] % length
    angles = phase_int.astype(jnp.float32) * (2.0 * math.pi / length)
    return jnp.stack([jnp.cos(angles), jnp.sin(angles)]).astype(jnp.bfloat16)


def masked_spectra(residual, offsets, radius, row_pos, length):
    freq_rows = signed_freq(row_pos, length)
    freq_cols = signed_freq(jnp.arange(length, dtype=jnp.int32), length)
    shift_rows = freq_rows[None, :] - offsets[:, 0:1]
    shift_cols = freq_cols[None, :] - offsets[:, 1:2]
    inside = shift_rows[:, :, None] ** 2 + shift_cols[:, None, :] ** 2 <= (radius**2)[:, None, None]
    return jnp.where(inside[:, None], residual, jnp.zeros_like(residual))


def select_depths(slice_order, depths):
    count = depths.shape[0]
    picker = (slice_order[:, None] == jnp.arange(count, dtype=jnp.int32)[None, :]).astype(
        jnp.float32
    )
    return jnp.dot(picker, depths, precision=lax.Precision.HIGHEST)


def mixing_weights(ordered, led_axial):
    phase_angle = ordered[:, None] * led_axial[None, :]
    cosine = jnp.cos(phase_angle)
    sine = jnp.sin(phase_angle)
    first = jnp.stack([cosine, sine], axis=-1)
    second = jnp.stack([-sine, cosine], axis=-1)
    return jnp.stack([first, second], axis=1).astype(jnp.bfloat16)


def apply_phase(summed, own_depths, axial):
    phase_angle = own_depths[:, None, None] * axial[None]
    cosine = jnp.cos(phase_angle)
    sine = jnp.sin(phase_angle)
    real_part = summed[:, 0] * cosine - summed[:, 1] * sine
    imag_part = summed[:, 0] * sine + summed[:, 1] * cosine
    return jnp.stack([real_part, imag_part], axis=1).astype(jnp.bfloat16)


def transform(spectra, out_pos, length, form):
    dft = dft_table(spectra.shape[-1], out_pos, length)
    products = jnp.einsum(form, spectra, dft, preferred_element_type=jnp.float32)
    real_part = products[:, 0, 0] - products[:, 1, 1]
    imag_part = products[:, 0, 1] + products[:, 1, 0]
    return jnp.stack([real_part, imag_part], axis=1)


def column_section(spectra, out_pos, length):
    out_count = out_pos.shape[0]
    block_size = min(256, out_count)
    pieces = [
        transform(spectra, out_pos[start : start + block_size], length, "jcak,tkm->jctma")
        for start in range(0, out_count, block_size)
    ]
    return jnp.concatenate(pieces, axis=2).astype(jnp.bfloat16)


def row_section(spectra, length):
    positions = jnp.arange(length, dtype=jnp.int32)
    block_size = min(256, length)
    pieces = [
        transform(spectra, positions[start : start + block_size], length, "jcak,tkm->jctam")
        for start in range(0, length, block_size)
    ]
    return jnp.concatenate(pieces, axis=3) * (1.0 / length)


def local(residual_spectra, led_offsets, pupil_radius, led_axial, depths, slice_order, axial):
    tile_rows = axial.shape[0]
    length = axial.shape[1]
    row_pos = lax.axis_index("tile") * tile_rows + jnp.arange(tile_rows, dtype=jnp.int32)
    masked = masked_spectra(residual_spectra, led_offsets, pupil_radius, row_pos, length)
    ordered = select_depths(slice_order, depths)
    weights = mixing_weights(ordered, led_axial)
    partial_value = jnp.einsum(
        "jolc,lcak->joak", weights, masked, preferred_element_type=jnp.float32
    )
    led_count = lax.axis_size("led")
    led_index = lax.axis_index("led")
    slice_count = depths.shape[0]
    summed = lax.psum_scatter(partial_value, "led", scatter_dimension=0, tiled=True)
    own_count = slice_count // led_count
    own_depths = lax.dynamic_slice_in_dim(ordered, led_index * own_count, own_count)
    phased = apply_phase(summed, own_depths, axial)
    half_done = column_section(phased, jnp.arange(length, dtype=jnp.int32), length)
    regrouped = lax.all_to_all(
        lax.all_to_all(half_done, "tile", split_axis=2, concat_axis=3, tiled=True),
        "led",
        split_axis=2,
        concat_axis=0,
        tiled=True,
    )
    gradient = row_section(regrouped, length)
    return gradient


def full_table(length):
    phase_int = np.outer(np.arange(length), np.arange(length)) % length
    angles = np.arange(length).astype(np.float64) * (2.0 * math.pi / length)
    pair = np.stack([np.cos(angles), np.sin(angles)]).astype(np.float32).astype(ml_dtypes.bfloat16)
    return pair[:, phase_int]


def useful_edge(length):
    reach = length // 6 + length // 4
    return -(-(reach + 1) // LANES) * LANES


def sine_cosine(angle):
    quarter = angle * 0.25
    z = quarter * quarter
    sine = quarter * (1.0 + z * (-1 / 6 + z * (1 / 120 + z * (-1 / 5040 + z * (1 / 362880)))))
    cosine = 1.0 + z * (
        -1 / 2 + z * (1 / 24 + z * (-1 / 720 + z * (1 / 40320 - z * (1 / 3628800))))
    )
    for _ in range(2):
        sine, cosine = 2.0 * sine * cosine, 1.0 - 2.0 * sine * sine
    return sine, cosine


def spread_weights(weights, spread):
    height, depth = weights.shape
    shape = (depth, depth * GROUP)
    picks = lax.broadcasted_iota(jnp.int32, shape, 1) // GROUP == lax.broadcasted_iota(
        jnp.int32, shape, 0
    )
    picks = jnp.where(picks, 1.0, 0.0).astype(jnp.bfloat16)
    wide = jnp.dot(weights[...], picks, preferred_element_type=jnp.float32)
    shape = (GROUP, depth * GROUP)
    diagonal = lax.broadcasted_iota(jnp.int32, shape, 1) % GROUP == lax.broadcasted_iota(
        jnp.int32, shape, 0
    )
    for row in range(height):
        block = jnp.where(diagonal, jnp.broadcast_to(wide[row : row + 1], shape), 0.0)
        spread[row * GROUP : (row + 1) * GROUP] = block.astype(jnp.bfloat16)


def mix_group(length, edge, row_start, ints, depths, spread, own, peer, axial, store):
    own_leds, peer_leds = own.shape[0], peer.shape[0]
    leds = own_leds + peer_leds
    slices = depths.shape[0]
    row = row_start + lax.broadcasted_iota(jnp.int32, (GROUP, 1), 0)
    freq_row = jnp.where(row < length // 2, row, row - length)
    lane = lax.broadcasted_iota(jnp.int32, (1, edge), 1)
    for half in range(2):
        start = 0 if half == 0 else length - edge
        freq_col = lane if half == 0 else lane - edge
        planes = []
        for led in range(leds):
            shift_row = freq_row - ints[led]
            shift_col = freq_col - ints[leds + led]
            room = ints[2 * leds + led] - shift_row * shift_row
            inside = jnp.where(shift_col * shift_col <= room, 1.0, 0.0).astype(jnp.bfloat16)
            for part in range(2):
                if led < own_leds:
                    values = own[led, part, :, start : start + edge]
                else:
                    values = peer[led - own_leds, part, :, half * edge : (half + 1) * edge]
                planes.append(values * inside)
        stacked = jnp.concatenate(planes, axis=0)
        summed = jnp.dot(spread[...], stacked, preferred_element_type=jnp.float32)
        wave = axial[:, start : start + edge]
        for j in range(slices):
            real = summed[(2 * j) * GROUP : (2 * j + 1) * GROUP]
            imag = summed[(2 * j + 1) * GROUP : (2 * j + 2) * GROUP]
            sine, cosine = sine_cosine(depths[j] * wave)
            where = slice(half * edge, (half + 1) * edge)
            store(j, 0, where, (real * cosine - imag * sine).astype(jnp.bfloat16))
            store(j, 1, where, (real * sine + imag * cosine).astype(jnp.bfloat16))


def transform_kernel(
    length,
    edge,
    ints,
    depths,
    weights,
    table_hbm,
    spectra_hbm,
    axial_hbm,
    out_hbm,
    table,
    phased,
    spread,
    own,
    peer,
    axial,
    send,
    recv,
    result,
    table_sem,
    own_sem,
    axial_sem,
    peer_send_sem,
    peer_recv_sem,
    send_sem,
    recv_sem,
    out_sem,
):
    slices = phased.shape[0]
    count = length // LANES
    dead_first, dead_last = edge // LANES, count - edge // LANES
    led_count = lax.axis_size("led")
    part = lax.axis_index("parts")
    me = lax.axis_index("tile") * led_count + lax.axis_index("led")

    def place(device):
        return (part, device // led_count, device % led_count)

    led_index = lax.axis_index("led")
    rows = axial.shape[0]
    first_row = me * rows
    steps = rows // GROUP
    quad = 4
    groups = count // quad
    partner = (part, me // led_count, 1 - led_index)

    def load_own(step):
        here = pl.ds(pl.multiple_of(led_index * rows + step * GROUP, GROUP), GROUP)
        return pltpu.make_async_copy(
            spectra_hbm.at[:, :, here], own.at[step % 2], own_sem.at[step % 2]
        )

    def load_axial():
        here = pl.ds(pl.multiple_of(led_index * rows, GROUP), rows)
        return pltpu.make_async_copy(axial_hbm.at[here], axial, axial_sem)

    def rows_of(group):
        return pl.ds(pl.multiple_of(group * quad * LANES, quad * LANES), quad * LANES)

    def load_table(step):
        there = rows_of((me // quad + groups // 2 + step) % groups)
        return pltpu.make_async_copy(
            table_hbm.at[:, there], table.at[:, there], table_sem.at[step]
        )

    def swap(step, half):
        there = pl.ds(pl.multiple_of((1 - led_index) * rows + step * GROUP, GROUP), GROUP)
        start = 0 if half == 0 else length - edge
        return pltpu.make_async_remote_copy(
            src_ref=spectra_hbm.at[:, :, there, start : start + edge],
            dst_ref=peer.at[step, :, :, :, half * edge : (half + 1) * edge],
            send_sem=peer_send_sem.at[step, half],
            recv_sem=peer_recv_sem.at[step, half],
            device_id=partner,
            device_id_type=MESH,
        )

    load_own(0).start()
    load_axial().start()

    barrier = pltpu.get_barrier_semaphore()

    @pl.loop(1, count)
    def _(step):
        pl.semaphore_signal(
            barrier, inc=1, device_id=place((me + step) % count), device_id_type=MESH
        )

    pl.semaphore_wait(barrier, count - 1)

    @pl.loop(0, steps)
    def _(step):
        swap(step, 0).start()
        swap(step, 1).start()

    @pl.loop(0, groups)
    def _(step):
        load_table(step).start()

    spread_weights(weights, spread)
    load_axial().wait()

    @pl.loop(0, steps)
    def _(step):
        @pl.when(step + 1 < steps)
        def _():
            load_own(step + 1).start()

        load_own(step).wait()
        swap(step, 0).wait_recv()
        swap(step, 1).wait_recv()
        here = pl.ds(pl.multiple_of(step * GROUP, GROUP), GROUP)

        def store(j, half, where, values):
            there = pl.ds(pl.multiple_of(half * rows + step * GROUP, GROUP), GROUP)
            phased[j, there, where] = values

        mix_group(
            length,
            edge,
            first_row + step * GROUP,
            ints,
            depths,
            spread,
            own.at[step % 2],
            peer.at[step],
            axial.at[here],
            store,
        )

    @pl.loop(0, groups)
    def _(step):
        load_table(step).wait()

    def lanes_of(device):
        return pl.ds(pl.multiple_of(device * LANES, LANES), LANES)

    def remote(j, device):
        return pltpu.make_async_remote_copy(
            src_ref=send.at[j, device],
            dst_ref=recv.at[j, :, lanes_of(me)],
            send_sem=send_sem.at[j, device],
            recv_sem=recv_sem.at[j, me],
            device_id=place(device),
            device_id_type=MESH,
        )

    def landing(j, device):
        return pltpu.make_async_copy(
            send.at[j, device], recv.at[j, :, lanes_of(device)], recv_sem.at[j, device]
        )

    has_rows = jnp.logical_or(me < dead_first, me >= dead_last)

    @pl.when(has_rows)
    def _():
        @pl.loop(0, slices)
        def _(j):
            spectra = phased[j]

            @pl.loop(0, groups)
            def _(step):
                group = (me // quad + groups // 2 + step) % groups
                here = rows_of(group)

                def product(t):
                    values = jnp.concatenate(
                        [table[t, here, :edge], table[t, here, length - edge :]], axis=1
                    )
                    return lax.dot_general(
                        values,
                        spectra,
                        (((1,), (1,)), ((), ())),
                        preferred_element_type=jnp.float32,
                    )

                by_cosine = product(0)
                by_sine = product(1)
                real = (by_cosine[:, :LANES] - by_sine[:, LANES:]).astype(jnp.bfloat16)
                imag = (by_sine[:, :LANES] + by_cosine[:, LANES:]).astype(jnp.bfloat16)
                for q in range(quad):
                    device = group * quad + q
                    send[j, device, :LANES] = real[q * LANES : (q + 1) * LANES]
                    send[j, device, LANES:] = imag[q * LANES : (q + 1) * LANES]

                    @pl.when(device == me)
                    def _():
                        landing(j, me).start()

                    @pl.when(device != me)
                    def _():
                        remote(j, device).start()

    width = 512

    def write(j):
        return pltpu.make_async_copy(result.at[j % 2], out_hbm.at[j], out_sem.at[j % 2])

    @pl.loop(0, slices)
    def _(j):
        @pl.loop(0, dead_first)
        def _(source):
            landing(j, source).wait()

        @pl.loop(dead_last, count)
        def _(source):
            landing(j, source).wait()

        @pl.when(j >= 2)
        def _():
            write(j - 2).wait()

        @pl.loop(0, length // width)
        def _(block):
            cols = pl.ds(pl.multiple_of(block * width, width), width)
            spectra = jnp.concatenate(
                [recv[j, :, :edge], recv[j, :, length - edge :]], axis=1
            )

            def product(t):
                values = jnp.concatenate(
                    [table[t, :edge, cols], table[t, length - edge :, cols]], axis=0
                )
                return jnp.dot(spectra, values, preferred_element_type=jnp.float32)

            by_cosine = product(0)
            by_sine = product(1)
            scale = 1.0 / length
            result[j % 2, 0, :, cols] = (by_cosine[:LANES] - by_sine[LANES:]) * scale
            result[j % 2, 1, :, cols] = (by_sine[:LANES] + by_cosine[LANES:]) * scale

        write(j).start()

    write(slices - 2).wait()
    write(slices - 1).wait()

    @pl.loop(0, steps)
    def _(step):
        swap(step, 0).wait_send()
        swap(step, 1).wait_send()

    @pl.when(has_rows)
    def _():
        @pl.loop(0, slices)
        def _(j):
            @pl.loop(1, count)
            def _(step):
                remote(j, (me + step) % count).wait_send()


def local_fast(residual_spectra, led_offsets, pupil_radius, led_axial, depths, slice_order, axial):
    tile_rows, length = axial.shape
    own_leds = residual_spectra.shape[0]
    slices = depths.shape[0]
    edge = useful_edge(length)
    rows = tile_rows // lax.axis_size("led")
    facts = jnp.concatenate(
        [led_offsets.astype(jnp.float32).T, pupil_radius.astype(jnp.float32)[None], led_axial[None]]
    )
    facts = jnp.concatenate([facts, lax.ppermute(facts, "led", [(0, 1), (1, 0)])], axis=1)
    leds = facts.shape[1]
    ordered = select_depths(slice_order, depths)
    weights = mixing_weights(ordered, facts[3]).reshape(2 * slices, 2 * leds)
    whole = facts[:3].astype(jnp.int32)
    ints = jnp.concatenate([whole[0], whole[1], whole[2] * whole[2]])
    count = length // LANES
    steps = rows // GROUP
    bf16 = jnp.bfloat16
    smem = pl.BlockSpec(memory_space=pltpu.SMEM)
    return pl.pallas_call(
        functools.partial(transform_kernel, length, edge),
        in_specs=[smem, smem, pl.BlockSpec(memory_space=pltpu.VMEM)]
        + [pl.BlockSpec(memory_space=pl.ANY)] * 3,
        out_specs=pl.BlockSpec(memory_space=pl.ANY),
        out_shape=jax.ShapeDtypeStruct((slices, 2, LANES, length), jnp.float32),
        scratch_shapes=[
            pltpu.VMEM((2, length, length), bf16),
            pltpu.VMEM((slices, 2 * rows, 2 * edge), bf16),
            pltpu.VMEM((2 * slices * GROUP, 2 * leds * GROUP), bf16),
            pltpu.VMEM((2, own_leds, 2, GROUP, length), bf16),
            pltpu.VMEM((steps, own_leds, 2, GROUP, 2 * edge), bf16),
            pltpu.VMEM((rows, length), jnp.float32),
            pltpu.VMEM((slices, count, 2 * LANES, LANES), bf16),
            pltpu.VMEM((slices, 2 * LANES, length), bf16),
            pltpu.VMEM((2, 2, LANES, length), jnp.float32),
            pltpu.SemaphoreType.DMA((count // 4,)),
            pltpu.SemaphoreType.DMA((2,)),
            pltpu.SemaphoreType.DMA,
            pltpu.SemaphoreType.DMA((steps, 2)),
            pltpu.SemaphoreType.DMA((steps, 2)),
            pltpu.SemaphoreType.DMA((slices, count)),
            pltpu.SemaphoreType.DMA((slices, count)),
            pltpu.SemaphoreType.DMA((2,)),
        ],
        compiler_params=pltpu.CompilerParams(
            collective_id=0, has_side_effects=True, vmem_limit_bytes=61 * 2**20
        ),
        name="transform",
    )(ints, ordered, weights, jnp.asarray(full_table(length)), residual_spectra, axial)


def local_any(*arrays):
    tile_rows, length = arrays[-1].shape
    led_count = lax.axis_size("led")
    if led_count == 2 and tile_rows == 2 * LANES and length % (8 * LANES) == 0:
        return local_fast(*arrays)
    return local(*arrays)


def solution(mesh):
    placed = (
        P(("parts", "led"), None, "tile", None),
        P("led", None),
        P("led"),
        P("led"),
        P(),
        P(),
        P("tile", None),
    )
    return jax.shard_map(
        local_any,
        mesh=mesh,
        in_specs=placed,
        out_specs=P("parts", None, ("tile", "led"), None),
        check_vma=False,
    )
```

```python
import functools
import math

import jax
import jax.numpy as jnp
import ml_dtypes
import numpy as np
from jax import lax
from jax.experimental import pallas as pl
from jax.experimental.pallas import tpu as pltpu
from jax.sharding import PartitionSpec as P

LANES = 128
GROUP = 16
MESH = pl.DeviceIdType.MESH


def signed_freq(index, length):
    return jnp.where(index < length // 2, index, index - length)


def dft_table(k_count, out_pos, length):
    k_index = jnp.arange(k_count, dtype=jnp.int32)
    phase_int = k_index[:, None] * out_pos[None, :] % length
    angles = phase_int.astype(jnp.float32) * (2.0 * math.pi / length)
    return jnp.stack([jnp.cos(angles), jnp.sin(angles)]).astype(jnp.bfloat16)


def masked_spectra(residual, offsets, radius, row_pos, length):
    freq_rows = signed_freq(row_pos, length)
    freq_cols = signed_freq(jnp.arange(length, dtype=jnp.int32), length)
    shift_rows = freq_rows[None, :] - offsets[:, 0:1]
    shift_cols = freq_cols[None, :] - offsets[:, 1:2]
    inside = shift_rows[:, :, None] ** 2 + shift_cols[:, None, :] ** 2 <= (radius**2)[:, None, None]
    return jnp.where(inside[:, None], residual, jnp.zeros_like(residual))


def select_depths(slice_order, depths):
    count = depths.shape[0]
    picker = (slice_order[:, None] == jnp.arange(count, dtype=jnp.int32)[None, :]).astype(
        jnp.float32
    )
    return jnp.dot(picker, depths, precision=lax.Precision.HIGHEST)


def mixing_weights(ordered, led_axial):
    phase_angle = ordered[:, None] * led_axial[None, :]
    cosine = jnp.cos(phase_angle)
    sine = jnp.sin(phase_angle)
    first = jnp.stack([cosine, sine], axis=-1)
    second = jnp.stack([-sine, cosine], axis=-1)
    return jnp.stack([first, second], axis=1).astype(jnp.bfloat16)


def apply_phase(summed, own_depths, axial):
    phase_angle = own_depths[:, None, None] * axial[None]
    cosine = jnp.cos(phase_angle)
    sine = jnp.sin(phase_angle)
    real_part = summed[:, 0] * cosine - summed[:, 1] * sine
    imag_part = summed[:, 0] * sine + summed[:, 1] * cosine
    return jnp.stack([real_part, imag_part], axis=1).astype(jnp.bfloat16)


def transform(spectra, out_pos, length, form):
    dft = dft_table(spectra.shape[-1], out_pos, length)
    products = jnp.einsum(form, spectra, dft, preferred_element_type=jnp.float32)
    real_part = products[:, 0, 0] - products[:, 1, 1]
    imag_part = products[:, 0, 1] + products[:, 1, 0]
    return jnp.stack([real_part, imag_part], axis=1)


def column_section(spectra, out_pos, length):
    out_count = out_pos.shape[0]
    block_size = min(256, out_count)
    pieces = [
        transform(spectra, out_pos[start : start + block_size], length, "jcak,tkm->jctma")
        for start in range(0, out_count, block_size)
    ]
    return jnp.concatenate(pieces, axis=2).astype(jnp.bfloat16)


def row_section(spectra, length):
    positions = jnp.arange(length, dtype=jnp.int32)
    block_size = min(256, length)
    pieces = [
        transform(spectra, positions[start : start + block_size], length, "jcak,tkm->jctam")
        for start in range(0, length, block_size)
    ]
    return jnp.concatenate(pieces, axis=3) * (1.0 / length)


def local(residual_spectra, led_offsets, pupil_radius, led_axial, depths, slice_order, axial):
    tile_rows = axial.shape[0]
    length = axial.shape[1]
    row_pos = lax.axis_index("tile") * tile_rows + jnp.arange(tile_rows, dtype=jnp.int32)
    masked = masked_spectra(residual_spectra, led_offsets, pupil_radius, row_pos, length)
    ordered = select_depths(slice_order, depths)
    weights = mixing_weights(ordered, led_axial)
    partial_value = jnp.einsum(
        "jolc,lcak->joak", weights, masked, preferred_element_type=jnp.float32
    )
    led_count = lax.axis_size("led")
    led_index = lax.axis_index("led")
    slice_count = depths.shape[0]
    summed = lax.psum_scatter(partial_value, "led", scatter_dimension=0, tiled=True)
    own_count = slice_count // led_count
    own_depths = lax.dynamic_slice_in_dim(ordered, led_index * own_count, own_count)
    phased = apply_phase(summed, own_depths, axial)
    half_done = column_section(phased, jnp.arange(length, dtype=jnp.int32), length)
    regrouped = lax.all_to_all(
        lax.all_to_all(half_done, "tile", split_axis=2, concat_axis=3, tiled=True),
        "led",
        split_axis=2,
        concat_axis=0,
        tiled=True,
    )
    gradient = row_section(regrouped, length)
    return gradient


def full_table(length):
    phase_int = np.outer(np.arange(length), np.arange(length)) % length
    angles = np.arange(length).astype(np.float64) * (2.0 * math.pi / length)
    pair = np.stack([np.cos(angles), np.sin(angles)]).astype(np.float32).astype(ml_dtypes.bfloat16)
    return pair[:, phase_int]


def useful_edge(length):
    reach = length // 6 + length // 4
    return -(-(reach + 1) // LANES) * LANES


def sine_cosine(angle):
    quarter = angle * 0.25
    z = quarter * quarter
    sine = quarter * (1.0 + z * (-1 / 6 + z * (1 / 120 + z * (-1 / 5040 + z * (1 / 362880)))))
    cosine = 1.0 + z * (
        -1 / 2 + z * (1 / 24 + z * (-1 / 720 + z * (1 / 40320 - z * (1 / 3628800))))
    )
    for _ in range(2):
        sine, cosine = 2.0 * sine * cosine, 1.0 - 2.0 * sine * sine
    return sine, cosine


def spread_weights(weights, spread):
    height, depth = weights.shape
    shape = (depth, depth * GROUP)
    picks = lax.broadcasted_iota(jnp.int32, shape, 1) // GROUP == lax.broadcasted_iota(
        jnp.int32, shape, 0
    )
    picks = jnp.where(picks, 1.0, 0.0).astype(jnp.bfloat16)
    wide = jnp.dot(weights[...], picks, preferred_element_type=jnp.float32)
    shape = (GROUP, depth * GROUP)
    diagonal = lax.broadcasted_iota(jnp.int32, shape, 1) % GROUP == lax.broadcasted_iota(
        jnp.int32, shape, 0
    )
    for row in range(height):
        block = jnp.where(diagonal, jnp.broadcast_to(wide[row : row + 1], shape), 0.0)
        spread[row * GROUP : (row + 1) * GROUP] = block.astype(jnp.bfloat16)


def mix_group(length, edge, row_start, ints, depths, spread, own, peer, axial, store):
    own_leds, peer_leds = own.shape[0], peer.shape[0]
    leds = own_leds + peer_leds
    slices = depths.shape[0]
    row = row_start + lax.broadcasted_iota(jnp.int32, (GROUP, 1), 0)
    freq_row = jnp.where(row < length // 2, row, row - length)
    lane = lax.broadcasted_iota(jnp.int32, (1, edge), 1)
    for half in range(2):
        start = 0 if half == 0 else length - edge
        freq_col = lane if half == 0 else lane - edge
        planes = []
        for led in range(leds):
            shift_row = freq_row - ints[led]
            shift_col = freq_col - ints[leds + led]
            room = ints[2 * leds + led] - shift_row * shift_row
            inside = jnp.where(shift_col * shift_col <= room, 1.0, 0.0).astype(jnp.bfloat16)
            for part in range(2):
                if led < own_leds:
                    values = own[led, part, :, start : start + edge]
                else:
                    values = peer[led - own_leds, part, :, half * edge : (half + 1) * edge]
                planes.append(values * inside)
        stacked = jnp.concatenate(planes, axis=0)
        summed = jnp.dot(spread[...], stacked, preferred_element_type=jnp.float32)
        wave = axial[:, start : start + edge]
        for j in range(slices):
            real = summed[(2 * j) * GROUP : (2 * j + 1) * GROUP]
            imag = summed[(2 * j + 1) * GROUP : (2 * j + 2) * GROUP]
            sine, cosine = sine_cosine(depths[j] * wave)
            where = slice(half * edge, (half + 1) * edge)
            store(j, 0, where, (real * cosine - imag * sine).astype(jnp.bfloat16))
            store(j, 1, where, (real * sine + imag * cosine).astype(jnp.bfloat16))


def transform_kernel(
    length,
    edge,
    ints,
    depths,
    weights,
    table_hbm,
    spectra_hbm,
    axial_hbm,
    out_hbm,
    table,
    phased,
    spread,
    own,
    peer,
    axial,
    send,
    recv,
    result,
    table_sem,
    own_sem,
    axial_sem,
    peer_send_sem,
    peer_recv_sem,
    send_sem,
    recv_sem,
    hand_send_sem,
    hand_recv_sem,
    out_sem,
):
    slices = phased.shape[0]
    count = length // LANES
    dead_first, dead_last = edge // LANES, count - edge // LANES
    half_count = count // 2
    handed_slices = slices // 2
    led_count = lax.axis_size("led")
    part = lax.axis_index("parts")
    me = lax.axis_index("tile") * led_count + lax.axis_index("led")

    def place(device):
        return (part, device // led_count, device % led_count)

    led_index = lax.axis_index("led")
    rows = axial.shape[0]
    first_row = me * rows
    steps = rows // GROUP
    quad = 4
    groups = count // quad
    partner = (part, me // led_count, 1 - led_index)

    def load_own(step):
        here = pl.ds(pl.multiple_of(led_index * rows + step * GROUP, GROUP), GROUP)
        return pltpu.make_async_copy(
            spectra_hbm.at[:, :, here], own.at[step % 2], own_sem.at[step % 2]
        )

    def load_axial():
        here = pl.ds(pl.multiple_of(led_index * rows, GROUP), rows)
        return pltpu.make_async_copy(axial_hbm.at[here], axial, axial_sem)

    def group_of(step):
        mine = me // quad
        return (mine // 2 + 1 + step // 2) % 2 * 2 + (mine + step + step // 2) % 2

    def rows_of(group):
        return pl.ds(pl.multiple_of(group * quad * LANES, quad * LANES), quad * LANES)

    def load_table(step):
        there = rows_of(group_of(step))
        return pltpu.make_async_copy(
            table_hbm.at[:, there], table.at[:, there], table_sem.at[step]
        )

    def swap(step, half):
        there = pl.ds(pl.multiple_of((1 - led_index) * rows + step * GROUP, GROUP), GROUP)
        start = 0 if half == 0 else length - edge
        return pltpu.make_async_remote_copy(
            src_ref=spectra_hbm.at[:, :, there, start : start + edge],
            dst_ref=peer.at[step, :, :, :, half * edge : (half + 1) * edge],
            send_sem=peer_send_sem.at[step, half],
            recv_sem=peer_recv_sem.at[step, half],
            device_id=partner,
            device_id_type=MESH,
        )

    load_own(0).start()
    load_axial().start()

    barrier = pltpu.get_barrier_semaphore()

    @pl.loop(1, count)
    def _(step):
        pl.semaphore_signal(
            barrier, inc=1, device_id=place((me + step) % count), device_id_type=MESH
        )

    pl.semaphore_wait(barrier, count - 1)

    @pl.loop(0, steps)
    def _(step):
        swap(step, 0).start()
        swap(step, 1).start()

    @pl.loop(0, groups)
    def _(step):
        load_table(step).start()

    spread_weights(weights, spread)
    load_axial().wait()

    @pl.loop(0, steps)
    def _(step):
        @pl.when(step + 1 < steps)
        def _():
            load_own(step + 1).start()

        load_own(step).wait()
        swap(step, 0).wait_recv()
        swap(step, 1).wait_recv()
        here = pl.ds(pl.multiple_of(step * GROUP, GROUP), GROUP)

        def store(j, half, where, values):
            there = pl.ds(pl.multiple_of(half * rows + step * GROUP, GROUP), GROUP)
            phased[j, there, where] = values

        mix_group(
            length,
            edge,
            first_row + step * GROUP,
            ints,
            depths,
            spread,
            own.at[step % 2],
            peer.at[step],
            axial.at[here],
            store,
        )

    @pl.loop(0, groups)
    def _(step):
        load_table(step).wait()

    def lanes_of(device):
        return pl.ds(pl.multiple_of(device * LANES, LANES), LANES)

    def remote(j, device):
        return pltpu.make_async_remote_copy(
            src_ref=send.at[j, device],
            dst_ref=recv.at[j, :, lanes_of(me)],
            send_sem=send_sem.at[j, device],
            recv_sem=recv_sem.at[j, me],
            device_id=place(device),
            device_id_type=MESH,
        )

    def landing(j, device):
        return pltpu.make_async_copy(
            send.at[j, device], recv.at[j, :, lanes_of(device)], recv_sem.at[j, device]
        )

    side = me // half_count
    far = pl.multiple_of((1 - side) * half_count, half_count)
    carrier = dead_first + side
    sender = carrier - 2 + 4 * side
    is_sender = me == sender
    is_carrier = me == carrier

    def hand_over(j):
        return pltpu.make_async_remote_copy(
            src_ref=send.at[j, pl.ds(far, half_count)],
            dst_ref=send.at[j, pl.ds(far, half_count)],
            send_sem=hand_send_sem.at[j],
            recv_sem=hand_recv_sem.at[j],
            device_id=place(carrier),
            device_id_type=MESH,
        )

    def handed(j):
        return pltpu.make_async_copy(
            send.at[j, pl.ds(far, half_count)],
            send.at[j, pl.ds(far, half_count)],
            hand_recv_sem.at[j],
        )

    def forward(j, device):
        return pltpu.make_async_remote_copy(
            src_ref=send.at[j, device],
            dst_ref=recv.at[j, :, lanes_of(sender)],
            send_sem=send_sem.at[j, device],
            recv_sem=recv_sem.at[j, sender],
            device_id=place(device),
            device_id_type=MESH,
        )

    has_rows = jnp.logical_or(me < dead_first, me >= dead_last)

    @pl.when(has_rows)
    def _():
        @pl.loop(0, slices)
        def _(j):
            spectra = phased[j]
            hands = jnp.logical_and(is_sender, j < handed_slices)

            @pl.loop(0, groups)
            def _(step):
                group = group_of(step)
                here = rows_of(group)

                def product(t):
                    values = jnp.concatenate(
                        [table[t, here, :edge], table[t, here, length - edge :]], axis=1
                    )
                    return lax.dot_general(
                        values,
                        spectra,
                        (((1,), (1,)), ((), ())),
                        preferred_element_type=jnp.float32,
                    )

                by_cosine = product(0)
                by_sine = product(1)
                real = (by_cosine[:, :LANES] - by_sine[:, LANES:]).astype(jnp.bfloat16)
                imag = (by_sine[:, :LANES] + by_cosine[:, LANES:]).astype(jnp.bfloat16)
                for q in range(quad):
                    device = group * quad + q
                    send[j, device, :LANES] = real[q * LANES : (q + 1) * LANES]
                    send[j, device, LANES:] = imag[q * LANES : (q + 1) * LANES]

                    @pl.when(device == me)
                    def _():
                        landing(j, me).start()

                    @pl.when(
                        jnp.logical_and(
                            device != me, jnp.logical_not(jnp.logical_and(hands, step < 2))
                        )
                    )
                    def _():
                        remote(j, device).start()

                @pl.when(jnp.logical_and(hands, step == 1))
                def _():
                    hand_over(j).start()

    @pl.when(is_carrier)
    def _():
        @pl.loop(0, handed_slices)
        def _(j):
            handed(j).wait()

            @pl.loop(0, half_count)
            def _(device):
                forward(j, far + device).start()

    width = 512

    def write(j):
        return pltpu.make_async_copy(result.at[j % 2], out_hbm.at[j], out_sem.at[j % 2])

    @pl.loop(0, slices)
    def _(j):
        @pl.loop(0, dead_first)
        def _(source):
            landing(j, source).wait()

        @pl.loop(dead_last, count)
        def _(source):
            landing(j, source).wait()

        @pl.when(j >= 2)
        def _():
            write(j - 2).wait()

        @pl.loop(0, length // width)
        def _(block):
            cols = pl.ds(pl.multiple_of(block * width, width), width)
            spectra = jnp.concatenate(
                [recv[j, :, :edge], recv[j, :, length - edge :]], axis=1
            )

            def product(t):
                values = jnp.concatenate(
                    [table[t, :edge, cols], table[t, length - edge :, cols]], axis=0
                )
                return jnp.dot(spectra, values, preferred_element_type=jnp.float32)

            by_cosine = product(0)
            by_sine = product(1)
            scale = 1.0 / length
            result[j % 2, 0, :, cols] = (by_cosine[:LANES] - by_sine[LANES:]) * scale
            result[j % 2, 1, :, cols] = (by_sine[:LANES] + by_cosine[LANES:]) * scale

        write(j).start()

    write(slices - 2).wait()
    write(slices - 1).wait()

    @pl.loop(0, steps)
    def _(step):
        swap(step, 0).wait_send()
        swap(step, 1).wait_send()

    @pl.when(has_rows)
    def _():
        @pl.loop(0, slices)
        def _(j):
            hands = jnp.logical_and(is_sender, j < handed_slices)

            @pl.loop(1, count)
            def _(step):
                device = (me + step) % count

                @pl.when(jnp.logical_not(jnp.logical_and(hands, device // half_count != side)))
                def _():
                    remote(j, device).wait_send()

            @pl.when(hands)
            def _():
                hand_over(j).wait_send()

    @pl.when(is_carrier)
    def _():
        @pl.loop(0, handed_slices)
        def _(j):
            @pl.loop(0, half_count)
            def _(device):
                forward(j, far + device).wait_send()


def local_fast(residual_spectra, led_offsets, pupil_radius, led_axial, depths, slice_order, axial):
    tile_rows, length = axial.shape
    own_leds = residual_spectra.shape[0]
    slices = depths.shape[0]
    edge = useful_edge(length)
    rows = tile_rows // lax.axis_size("led")
    facts = jnp.concatenate(
        [led_offsets.astype(jnp.float32).T, pupil_radius.astype(jnp.float32)[None], led_axial[None]]
    )
    facts = jnp.concatenate([facts, lax.ppermute(facts, "led", [(0, 1), (1, 0)])], axis=1)
    leds = facts.shape[1]
    ordered = select_depths(slice_order, depths)
    weights = mixing_weights(ordered, facts[3]).reshape(2 * slices, 2 * leds)
    whole = facts[:3].astype(jnp.int32)
    ints = jnp.concatenate([whole[0], whole[1], whole[2] * whole[2]])
    count = length // LANES
    steps = rows // GROUP
    bf16 = jnp.bfloat16
    smem = pl.BlockSpec(memory_space=pltpu.SMEM)
    return pl.pallas_call(
        functools.partial(transform_kernel, length, edge),
        in_specs=[smem, smem, pl.BlockSpec(memory_space=pltpu.VMEM)]
        + [pl.BlockSpec(memory_space=pl.ANY)] * 3,
        out_specs=pl.BlockSpec(memory_space=pl.ANY),
        out_shape=jax.ShapeDtypeStruct((slices, 2, LANES, length), jnp.float32),
        scratch_shapes=[
            pltpu.VMEM((2, length, length), bf16),
            pltpu.VMEM((slices, 2 * rows, 2 * edge), bf16),
            pltpu.VMEM((2 * slices * GROUP, 2 * leds * GROUP), bf16),
            pltpu.VMEM((2, own_leds, 2, GROUP, length), bf16),
            pltpu.VMEM((steps, own_leds, 2, GROUP, 2 * edge), bf16),
            pltpu.VMEM((rows, length), jnp.float32),
            pltpu.VMEM((slices, count, 2 * LANES, LANES), bf16),
            pltpu.VMEM((slices, 2 * LANES, length), bf16),
            pltpu.VMEM((2, 2, LANES, length), jnp.float32),
            pltpu.SemaphoreType.DMA((count // 4,)),
            pltpu.SemaphoreType.DMA((2,)),
            pltpu.SemaphoreType.DMA,
            pltpu.SemaphoreType.DMA((steps, 2)),
            pltpu.SemaphoreType.DMA((steps, 2)),
            pltpu.SemaphoreType.DMA((slices, count)),
            pltpu.SemaphoreType.DMA((slices, count)),
            pltpu.SemaphoreType.DMA((slices,)),
            pltpu.SemaphoreType.DMA((slices,)),
            pltpu.SemaphoreType.DMA((2,)),
        ],
        compiler_params=pltpu.CompilerParams(
            collective_id=0, has_side_effects=True, vmem_limit_bytes=61 * 2**20
        ),
        name="transform",
    )(ints, ordered, weights, jnp.asarray(full_table(length)), residual_spectra, axial)


def local_any(*arrays):
    tile_rows, length = arrays[-1].shape
    led_count = lax.axis_size("led")
    if led_count == 2 and tile_rows == 2 * LANES and length == 16 * LANES:
        return local_fast(*arrays)
    return local(*arrays)


def solution(mesh):
    placed = (
        P(("parts", "led"), None, "tile", None),
        P("led", None),
        P("led"),
        P("led"),
        P(),
        P(),
        P("tile", None),
    )
    return jax.shard_map(
        local_any,
        mesh=mesh,
        in_specs=placed,
        out_specs=P("parts", None, ("tile", "led"), None),
        check_vma=False,
    )
```
